32 devices in a mesh: col: 4 (over z), leaf: 8 (over y, x, core).
Axes of the slice: x: 2, y: 2, z: 4, core: 2. Of those that a mesh axis runs over, the one named last changes fastest.
Arguments:
- voltage: bfloat16 [128, 32, 4, 1024], P(None, 'leaf', None, 'col'), may hold values from -4 to 4
- source: bfloat16 [128, 32, 4, 1024], P(None, 'leaf', None, 'col'), may hold values from -6 to 6
- conduct: float32 [32, 4, 1024], P('leaf', None, 'col'), may hold values from 0.25 to 2
- leaf_inverse: bfloat16 [32, 4, 1024, 256], P('leaf', None, 'col'), as said below
- update_rows: int32 [4, 32, 4, 2], P('col', 'leaf'), may hold values from 0 to 31, as said below
- update_matrix: bfloat16 [32, 4, 256, 1024], P('leaf', None, None, 'col'), may hold values from -0.1875 to 0.1875
- chain_slot: int32 [16], replicated, may hold values from 0 to 15, as said below
- separator_source: float32 [128, 16, 1024], P(None, 'leaf', 'col'), may hold values from -6 to 6
- separator_inverse: float32 [16, 1024, 256], P('leaf', 'col'), as said below
- separator_coupling: float32 [16, 1024, 256], P('leaf', 'col'), may hold values from -0.3125 to 0.3125
Outputs:
- leaf_result: float32 [128, 32, 4, 1024], P(None, 'leaf', None, 'col')
- separator_result: float32 [128, 16, 1024], P(None, 'leaf', 'col')
The draws below stay inside these ranges and needn't reach their ends.
Inputs may be any that keep to these rules, and one draw needn't show every extreme that they name: `update_rows`: row [q, x, y] names 2 different update-row blocks of the separator panels at position q; block t holds rows (t % 2) * 128 onward of chain t // 2. Among the 32 entries of the rows [q, x, y] held by one device, at most 4 name blocks whose chains are stored in storage rows i * 2 to (i + 1) * 2 - 1 for one i, and exactly 4 do for some i on every device. A permutation: chain j is stored at row chain_slot[j] of the separator arrays. `leaf_inverse`: each 256 x 256 block is a given inverse of a diagonal block. `separator_inverse`: each 256 x 256 block is a given inverse of a diagonal block.
All inputs are finite; a program needn't handle non-finite values.
Results may differ from the reference program's by a relative error of at most 0.0039.
Values may be sent and summed in bfloat16 or wider, within the bound.
A program may use at most 128 MiB of HBM per device.

```python
import math
import jax
import jax.numpy as jnp
from jax import lax

NRHS = 128
CX = 4
CY = 4
PANEL = 256
BLK = 128
K = 2
SEP_DEV = 2
NX = 32
NY = 4
NZ = 1024
SCHAIN = 16
NSEP = 1024
CAP = 4
N_COL = 4


def inverse_blocks(key, shape):
    rows = lax.broadcasted_iota(jnp.int32, shape, len(shape) - 2) % PANEL
    cols = lax.broadcasted_iota(jnp.int32, shape, len(shape) - 1)
    first_key, second_key = jax.random.split(key)
    diag_part = jnp.exp(jax.random.uniform(first_key, shape, jnp.float32, math.log(0.5), math.log(2.0)))
    off_part = jax.random.normal(second_key, shape, jnp.float32) * (0.5 / math.sqrt(PANEL))
    return jnp.where(rows == cols, diag_part, off_part)


def draw_leaf_inverse(key, part):
    return inverse_blocks(jax.random.fold_in(key, 11), (NX, NY, NZ, PANEL)).astype(jnp.bfloat16)


def draw_separator_inverse(key, part):
    return inverse_blocks(jax.random.fold_in(key, 23), (SCHAIN, NSEP, PANEL)).astype(jnp.float32)


def routing_tables(key):
    base = jax.random.fold_in(key, 77)
    order_key, owner_key, offset_key = jax.random.split(base, 3)
    leaves = NX // CX
    columns = NZ // PANEL
    halves = PANEL // BLK
    local_targets = SEP_DEV * halves
    order_score = jax.random.randint(order_key, (SCHAIN,), 0, 1 << 20, jnp.int32) * SCHAIN + jnp.arange(SCHAIN, dtype=jnp.int32)
    chain_of_slot = jnp.argsort(order_score, stable=True).astype(jnp.int32)
    slot_of_chain = jnp.argsort(chain_of_slot, stable=True).astype(jnp.int32)
    owner_score = jax.random.randint(owner_key, (columns, leaves, leaves), 0, 1 << 20, jnp.int32) * leaves + lax.broadcasted_iota(jnp.int32, (columns, leaves, leaves), 2)
    owner_order = jnp.argsort(owner_score, axis=2, stable=True).astype(jnp.int32)
    offsets = jax.random.randint(offset_key, (columns, leaves, leaves), 0, local_targets, jnp.int32)
    entry = jnp.arange(CX * CY * K, dtype=jnp.int32)
    group = entry // CAP
    within = entry % CAP
    owner = owner_order[:, :, group]
    local = (offsets[:, :, group] + within) % local_targets
    slot = owner * SEP_DEV + local // halves
    targets = chain_of_slot[slot] * halves + local % halves
    rows = targets.reshape(columns, leaves * CX, CY, K).astype(jnp.int32)
    return (rows, slot_of_chain)


def draw_update_rows(key, part):
    rows, slot_of_chain = routing_tables(key)
    return rows


def draw_chain_slot(key, part):
    rows, slot_of_chain = routing_tables(key)
    return slot_of_chain


def levels(rng, shape, pieces, low, largest):
    def one(axis_at, shards_of):
        draws = jax.random.uniform(jax.random.fold_in(jax.random.fold_in(rng, 6), axis_at), (shards_of,), jnp.float32, low / len(pieces), largest / len(pieces))
        return jnp.repeat(jnp.exp(draws), shape[axis_at] // shards_of).reshape((-1,) + (1,) * (len(shape) - axis_at - 1))

    gain = one(*pieces[0])
    for cut in pieces[1:]:
        gain = gain * one(*cut)
    return gain


def gaussian(stream_key, extent, deviation, limit, shards=(), kind=jnp.bfloat16):
    drawn = deviation * jax.random.normal(stream_key, extent, jnp.float32)
    if shards:
        drawn = drawn * levels(stream_key, extent, shards, -0.22, 0.18)
    return jnp.clip(drawn, -limit, limit).astype(kind)


def setup_inputs(seed: int = 0) -> dict:
    arg_keys = jax.random.split(jax.random.key(seed), 11)
    voltage = gaussian(arg_keys[0], (NRHS, NX, NY, NZ), 0.3, 4.0, ((1, 8), (3, 4)))
    source = gaussian(arg_keys[1], (NRHS, NX, NY, NZ), 1.0, 6.0, ((1, 8), (3, 4)))
    conduct = jnp.clip(0.25 + 1.75 * jax.random.uniform(arg_keys[2], (NX, NY, NZ), jnp.float32) ** levels(arg_keys[2], (NX, NY, NZ), ((0, 8), (2, 4)), -0.2, 0.2), 0.25, 2.0)
    leaf_inverse = draw_leaf_inverse(jax.random.fold_in(arg_keys[10], 71), 0)
    update_rows = draw_update_rows(jax.random.fold_in(arg_keys[10], 71), 0)
    update_matrix = gaussian(arg_keys[5], (NX, NY, K * BLK, NZ), (4 * PANEL) ** -0.5, 0.1875, ((0, 8), (3, 4)))
    chain_slot = draw_chain_slot(jax.random.fold_in(arg_keys[10], 71), 0)
    separator_source = gaussian(arg_keys[7], (NRHS, SCHAIN, NSEP), 1.0, 6.0, ((1, 8), (2, 4)), jnp.float32)
    separator_inverse = draw_separator_inverse(jax.random.fold_in(arg_keys[10], 71), 0)
    separator_coupling = gaussian(arg_keys[9], (SCHAIN, NSEP, PANEL), (PANEL * 3 // 2) ** -0.5, 0.3125, ((0, 8), (1, 4)), jnp.float32)
    return dict(voltage=voltage, source=source, conduct=conduct, leaf_inverse=leaf_inverse, update_rows=update_rows, update_matrix=update_matrix, chain_slot=chain_slot, separator_source=separator_source, separator_inverse=separator_inverse, separator_coupling=separator_coupling)


def reference(voltage, source, conduct, leaf_inverse, update_rows, update_matrix, chain_slot, separator_source, separator_inverse, separator_coupling):
    highest = lax.Precision.HIGHEST
    fields = voltage.shape[0]
    halves = PANEL // BLK
    volt_wide = voltage.astype(jnp.float32)
    padded = jnp.pad(volt_wide, ((0, 0), (1, 1), (1, 1), (1, 1)))
    beside = padded[:, 2:, 1:-1, 1:-1] + padded[:, :-2, 1:-1, 1:-1]
    beside = beside + padded[:, 1:-1, 2:, 1:-1] + padded[:, 1:-1, :-2, 1:-1]
    beside = beside + padded[:, 1:-1, 1:-1, 2:] + padded[:, 1:-1, 1:-1, :-2]
    residual = source.astype(jnp.float32) - ((6.0 + conduct) * volt_wide - beside)
    residual_low = residual.astype(jnp.bfloat16).reshape(fields, NX, NY, N_COL, PANEL)
    target_slot = chain_slot[update_rows // halves].astype(jnp.int32)
    target_half = update_rows % halves
    slot_x = jnp.moveaxis(target_slot, 1, 0)
    half_x = jnp.moveaxis(target_half, 1, 0)
    inverse_x = leaf_inverse.reshape(NX, NY, N_COL, PANEL, PANEL)
    matrix_x = update_matrix.reshape(NX, NY, K, BLK, N_COL, PANEL)
    residual_x = jnp.moveaxis(residual_low, 1, 0)

    def make_picker(slots, halfs):
        slot_hit = (slots[..., None] == jnp.arange(SCHAIN, dtype=jnp.int32)).astype(jnp.float32)
        half_hit = (halfs[..., None] == jnp.arange(halves, dtype=jnp.int32)).astype(jnp.float32)
        return slot_hit[..., :, None] * half_hit[..., None, :]

    def forward_step(dense, slices):
        resid_now, inverse_now, matrix_now, slots, halfs = slices
        resid_wide = resid_now.astype(jnp.float32)
        scaled = jnp.einsum("yqab,nyqb->nyqa", inverse_now.astype(jnp.float32), resid_wide, precision=highest)
        contrib = jnp.einsum("ykjqb,nyqb->qyknj", matrix_now.astype(jnp.float32), resid_wide, precision=highest)
        picker = make_picker(slots, halfs)
        dense = dense + jnp.einsum("qyksh,qyknj->nsqhj", picker, contrib, precision=highest)
        return dense, scaled

    dense_init = jnp.zeros((fields, SCHAIN, N_COL, halves, BLK), jnp.float32)
    dense, leaf_scaled = lax.scan(forward_step, dense_init, (residual_x, inverse_x, matrix_x, slot_x, half_x))
    drive = separator_source.reshape(fields, SCHAIN, N_COL, PANEL) - dense.reshape(fields, SCHAIN, N_COL, PANEL)
    coupling = separator_coupling.reshape(SCHAIN, N_COL, PANEL, PANEL)
    sep_inverse = separator_inverse.reshape(SCHAIN, N_COL, PANEL, PANEL)
    forward_values = []
    previous = None
    for column in range(N_COL):
        current = drive[:, :, column]
        if column > 0:
            current = current - jnp.einsum("eab,neb->nea", coupling[:, column], previous, precision=highest)
        forward_values.append(current)
        previous = current
    scaled_sep = [jnp.einsum("eab,neb->nea", sep_inverse[:, column], forward_values[column], precision=highest) for column in range(N_COL)]
    results = [None] * N_COL
    following = None
    for column in reversed(range(N_COL)):
        current = scaled_sep[column]
        if column < N_COL - 1:
            current = current - jnp.einsum("eba,neb->nea", coupling[:, column + 1], following, precision=highest)
        results[column] = current
        following = current
    separator_result = jnp.stack(results, axis=2).reshape(fields, SCHAIN, NSEP)
    separator_low = separator_result.astype(jnp.bfloat16).reshape(fields, SCHAIN, N_COL, halves, BLK).astype(jnp.float32)

    def backward_step(slices):
        scaled_now, matrix_now, slots, halfs = slices
        picker = make_picker(slots, halfs)
        picked = jnp.einsum("qyksh,nsqhj->qyknj", picker, separator_low, precision=highest)
        correction = jnp.einsum("ykjqb,qyknj->nyqb", matrix_now.astype(jnp.float32), picked, precision=highest)
        return scaled_now - correction

    leaf_out = lax.map(backward_step, (leaf_scaled, matrix_x, slot_x, half_x))
    leaf_result = jnp.moveaxis(leaf_out, 0, 1).reshape(fields, NX, NY, NZ)
    return leaf_result, separator_result
```

```python
import functools
import jax
import jax.numpy as jnp
from jax import lax
from jax.experimental import pallas as pl
from jax.experimental.pallas import tpu as pltpu
from jax.sharding import PartitionSpec as P

F32 = jnp.float32
BF16 = jnp.bfloat16
SPLIT = 2
PAIR = F32
HOP = BF16
NT = (((1,), (1,)), ((), ()))
NN = (((1,), (0,)), ((), ()))


def flipped(value, bits, count):
    total = 0
    weight = 1
    while weight < count:
        digit = (value // weight) % 2
        total = total + weight * (1 - digit if (bits // weight) % 2 else digit)
        weight *= 2
    return total


def dot(left, right, dims):
    return lax.dot_general(left, right, dims, preferred_element_type=F32)


def halved(value):
    high = value.astype(BF16)
    return high, (value - high.astype(F32)).astype(BF16)


def kernel(
    n_leaf, n_col, cap, extent_x, extent_y, sep_rows, halves,
    tab, v, s, cond, sep, inv_hbm, upd_hbm, sinv_hbm, coup_hbm,
    out, res,
    inv, upd, sinv, coup, c_hi, c_lo, d_hi, d_lo,
    resid, contrib, z_send, z_recv, x_recv,
    pair_send, pair_recv, keep, chip_send, chip_recv,
    drive, f_send, f_recv, scaled, b_send, b_recv, gath,
    load_sem, zs_sem, zr_sem, xs_sem, xr_sem, ps_sem, pr_sem, cs_sem, cr_sem,
    fs_sem, fr_sem, bs_sem, br_sem, gs_sem, gr_sem, hs_sem, hr_sem,
):
    panels, fields, width = v.shape
    block = width // halves
    local = sep_rows * halves
    chips = n_leaf // 2
    leaf = lax.axis_index("leaf")
    col = lax.axis_index("col")
    core = leaf % 2
    chip = leaf // 2
    sibling = chip * 2 + (1 - core)
    entries = 2 * panels
    owners_cap = n_leaf * cap
    MESH = pl.DeviceIdType.MESH

    def remote(src, dst, send, recv, target):
        return pltpu.make_async_remote_copy(
            src_ref=src, dst_ref=dst, send_sem=send, recv_sem=recv,
            device_id=target, device_id_type=MESH,
        )

    loads = [
        pltpu.make_async_copy(src, dst, load_sem.at[i])
        for i, (src, dst) in enumerate(
            ((upd_hbm, upd), (inv_hbm, inv), (coup_hbm, coup), (sinv_hbm, sinv))
        )
    ]
    for load in loads:
        load.start()

    barrier = pltpu.get_barrier_semaphore()
    for step in range(1, n_leaf):
        pl.semaphore_signal(
            barrier, inc=1, device_id={"leaf": (leaf + step) % n_leaf}, device_id_type=MESH
        )
    has_below, has_above = col > 0, col < n_col - 1
    leaf_below, leaf_above = leaf > 0, leaf < n_leaf - 1

    @pl.when(has_below)
    def _():
        pl.semaphore_signal(barrier, inc=1, device_id={"col": col - 1}, device_id_type=MESH)

    @pl.when(has_above)
    def _():
        pl.semaphore_signal(barrier, inc=1, device_id={"col": col + 1}, device_id_type=MESH)

    lane = lax.broadcasted_iota(jnp.int32, (fields, 128), 1)
    first = jnp.zeros((fields, 128), F32)
    last = jnp.zeros((fields, 128), F32)
    for p in range(panels):
        first = jnp.where(lane == p, v[p, :, 0:128].astype(F32)[:, 0:1], first)
        last = jnp.where(lane == p, v[p, :, width - 128:].astype(F32)[:, 127:128], last)
    z_send[0] = first.astype(BF16)
    z_send[1] = last.astype(BF16)

    beside_col = (col + n_col - 1) // n_col + (2 * n_col - 2 - col) // n_col
    pl.semaphore_wait(barrier, n_leaf - 1 + beside_col)

    z_down = lambda: remote(z_send.at[0], z_recv.at[1], zs_sem.at[0], zr_sem.at[1], {"col": col - 1})
    z_up = lambda: remote(z_send.at[1], z_recv.at[0], zs_sem.at[1], zr_sem.at[0], {"col": col + 1})
    x_down = lambda: remote(
        v.at[pl.ds(0, extent_y)], x_recv.at[1], xs_sem.at[0], xr_sem.at[1], {"leaf": leaf - 1}
    )
    x_up = lambda: remote(
        v.at[pl.ds(panels - extent_y, extent_y)], x_recv.at[0], xs_sem.at[1], xr_sem.at[0],
        {"leaf": leaf + 1},
    )

    for has, copy in ((has_below, z_down), (has_above, z_up), (leaf_below, x_down), (leaf_above, x_up)):
        @pl.when(has)
        def _(copy=copy):
            copy().start()

    for has, ref, slot in (
        (has_below, z_recv, 0), (has_above, z_recv, 1), (leaf_below, x_recv, 0), (leaf_above, x_recv, 1),
    ):
        @pl.when(jnp.logical_not(has))
        def _(ref=ref, slot=slot):
            ref[slot] = jnp.zeros(ref.shape[1:], ref.dtype)

    @pl.when(has_below)
    def _():
        z_up().wait_recv()

    @pl.when(has_above)
    def _():
        z_down().wait_recv()

    loads[0].wait()
    wide_lane = lax.broadcasted_iota(jnp.int32, (fields, width), 1)

    def residual_panel(x, y):
        p = x * extent_y + y
        center = v[p].astype(F32)
        before = z_recv[0].astype(F32)[:, p:p + 1]
        after = z_recv[1].astype(F32)[:, p:p + 1]
        beside = jnp.where(wide_lane == 0, before, pltpu.roll(center, 1, 1))
        beside = beside + jnp.where(wide_lane == width - 1, after, pltpu.roll(center, width - 1, 1))
        beside = beside + (v[p - extent_y] if x > 0 else x_recv[0, y]).astype(F32)
        beside = beside + (v[p + extent_y] if x < extent_x - 1 else x_recv[1, y]).astype(F32)
        if y > 0:
            beside = beside + v[p - 1].astype(F32)
        if y < extent_y - 1:
            beside = beside + v[p + 1].astype(F32)
        low = (s[p].astype(F32) - ((6.0 + cond[p:p + 1, :]) * center - beside)).astype(BF16)
        resid[p] = low
        product = dot(low, upd[p], NT)
        contrib[2 * p] = product[:, :block]
        contrib[2 * p + 1] = product[:, block:]

    for x in range(1, extent_x - 1):
        for y in range(extent_y):
            residual_panel(x, y)

    @pl.when(leaf_below)
    def _():
        x_up().wait_recv()

    @pl.when(leaf_above)
    def _():
        x_down().wait_recv()

    for x in (0, extent_x - 1):
        for y in range(extent_y):
            residual_panel(x, y)

    def dense(owner, m):
        total = jnp.zeros((fields, block), F32)
        for r in range(cap):
            at = owner * cap + r
            weight = jnp.where(tab[owners_cap + at] == m, 1.0, 0.0).astype(F32)
            total = total + weight * contrib[tab[at]]
        return total

    order = list(range(chips - 1, -1, -1))
    peer_chip = [flipped(chip, d, chips) for d in range(chips)]

    def pair_copy(d):
        return remote(pair_send.at[d], pair_recv.at[d], ps_sem.at[d], pr_sem.at[d], {"leaf": sibling})

    def chip_copy(d):
        return remote(
            chip_send.at[d], chip_recv.at[d], cs_sem.at[d], cr_sem.at[d],
            {"leaf": peer_chip[d] * 2 + core},
        )

    for d in order:
        def fill(m, carry, d=d):
            pair_send[d, m] = dense(peer_chip[d] * 2 + (1 - core), m).astype(pair_send.dtype)
            return carry
        lax.fori_loop(0, local, fill, 0)
        pair_copy(d).start()
    for d in order:
        def fill_own(m, carry, d=d):
            keep[d, m] = dense(peer_chip[d] * 2 + core, m)
            return carry
        lax.fori_loop(0, local, fill_own, 0)
        pair_copy(d).wait_recv()
        if d > 0:
            chip_send[d] = (keep[d] + pair_recv[d].astype(F32)).astype(BF16)
            chip_copy(d).start()

    for load in loads[1:]:
        load.wait()

    def leaf_scale(p, carry):
        out[p] = dot(resid[p], inv[p], NT)
        return carry
    lax.fori_loop(0, panels, leaf_scale, 0)
    for e in range(sep_rows):
        c_hi[e], c_lo[e] = halved(coup[e])
        d_hi[e], d_lo[e] = halved(sinv[e])

    for e in range(sep_rows):
        for h in range(halves):
            m = e * halves + h
            lanes = slice(h * block, (h + 1) * block)
            drive[e, :, lanes] = sep[e, :, lanes] - (keep[0, m] + pair_recv[0, m].astype(F32))
    for d in order:
        if d > 0:
            chip_copy(d).wait_recv()
            for e in range(sep_rows):
                for h in range(halves):
                    lanes = slice(h * block, (h + 1) * block)
                    drive[e, :, lanes] = drive[e, :, lanes] - chip_recv[d, e * halves + h].astype(F32)

    rows_each = fields // SPLIT
    pieces = [(e, q) for e in range(sep_rows) for q in range(SPLIT)]

    def f_copy(i):
        return remote(f_send.at[i], f_recv.at[i], fs_sem.at[i], fr_sem.at[i], {"col": col + 1})

    def b_copy(i):
        return remote(b_send.at[i], b_recv.at[i], bs_sem.at[i], br_sem.at[i], {"col": col - 1})

    for i, (e, q) in enumerate(pieces):
        rows = slice(q * rows_each, (q + 1) * rows_each)

        @pl.when(has_below)
        def _(i=i, e=e, rows=rows):
            f_copy(i).wait_recv()
            drive[e, rows] = drive[e, rows] - (
                dot(f_recv[i], c_hi[e], NT) + dot(f_recv[i], c_lo[e], NT)
            )

        @pl.when(has_above)
        def _(i=i, e=e, rows=rows):
            f_send[i] = drive[e, rows].astype(BF16)
            f_copy(i).start()

        high, low = halved(drive[e, rows])
        scaled[e, rows] = dot(high, d_hi[e], NT) + dot(high, d_lo[e], NT) + dot(low, d_hi[e], NT)

    def spot(owner_leaf, e):
        return pl.ds((owner_leaf * sep_rows + e) * halves, halves)

    def gather_copy(d, e):
        here = gath.at[spot(leaf, e)]
        return remote(here, here, gs_sem.at[d, e], gr_sem.at[d, e], {"leaf": peer_chip[d] * 2 + core})

    def hand_copy(d, e):
        here = gath.at[spot(peer_chip[d] * 2 + core, e)]
        return remote(here, here, hs_sem.at[d, e], hr_sem.at[d, e], {"leaf": sibling})

    for i, (e, q) in enumerate(pieces):
        rows = slice(q * rows_each, (q + 1) * rows_each)

        @pl.when(has_above)
        def _(i=i, e=e, rows=rows):
            b_copy(i).wait_recv()
            scaled[e, rows] = scaled[e, rows] - b_recv[i].astype(F32)

        value = scaled[e, rows]
        low = value.astype(BF16)

        @pl.when(has_below)
        def _(i=i, e=e, value=value, low=low):
            rest = (value - low.astype(F32)).astype(BF16)
            up = dot(low, c_hi[e], NN) + dot(low, c_lo[e], NN) + dot(rest, c_hi[e], NN)
            b_send[i] = up.astype(b_send.dtype)
            b_copy(i).start()

        res[e, rows] = value
        for h in range(halves):
            gath[(leaf * sep_rows + e) * halves + h, rows] = low[:, h * block:(h + 1) * block]
        if q == SPLIT - 1:
            for d in order:
                if d > 0:
                    gather_copy(d, e).start()
            hand_copy(0, e).start()

    for e in range(sep_rows):
        for d in range(1, chips):
            gather_copy(d, e).wait_recv()
            hand_copy(d, e).start()
    for e in range(sep_rows):
        for d in range(chips):
            hand_copy(d, e).wait_recv()

    def correct(p, carry):
        one = gath[tab[2 * owners_cap + 2 * p]]
        two = gath[tab[2 * owners_cap + 2 * p + 1]]
        out[p] = out[p] - (dot(one, upd[p, :block], NN) + dot(two, upd[p, block:], NN))
        return carry
    lax.fori_loop(0, panels, correct, 0)

    for has, copy in ((has_below, z_down), (has_above, z_up), (leaf_below, x_down), (leaf_above, x_up)):
        @pl.when(has)
        def _(copy=copy):
            copy().wait_send()
    for i in range(len(pieces)):
        @pl.when(has_above)
        def _(i=i):
            f_copy(i).wait_send()

        @pl.when(has_below)
        def _(i=i):
            b_copy(i).wait_send()
    for d in range(chips):
        pair_copy(d).wait_send()
        if d > 0:
            chip_copy(d).wait_send()
        for e in range(sep_rows):
            hand_copy(d, e).wait_send()
            if d > 0:
                gather_copy(d, e).wait_send()


def body(
    voltage,
    source,
    conduct,
    leaf_inverse,
    update_rows,
    update_matrix,
    chain_slot,
    separator_source,
    separator_inverse,
    separator_coupling,
):
    fields, extent_x, extent_y, width = voltage.shape
    per_leaf = update_rows.shape[3]
    block = update_matrix.shape[2] // per_leaf
    halves = width // block
    panels = extent_x * extent_y
    chains = chain_slot.shape[0]
    sep_rows = separator_source.shape[1]
    n_leaf, n_col = lax.axis_size("leaf"), lax.axis_size("col")
    chips = n_leaf // 2
    entries = panels * per_leaf
    cap = max(2, (entries + n_leaf - 1) // n_leaf)
    local = sep_rows * halves

    targets = update_rows.reshape(entries)
    hit = (targets // halves)[:, None] == jnp.arange(chains, dtype=jnp.int32)
    slots = jnp.sum(jnp.where(hit, chain_slot, 0), axis=1)
    blocks = slots * halves + targets % halves
    owner = slots // sep_rows
    ids = jnp.arange(entries, dtype=jnp.int32)
    earlier = (owner[:, None] == owner[None, :]) & (ids[None, :] < ids[:, None])
    rank = jnp.sum(earlier.astype(jnp.int32), axis=1)
    place = owner * cap + rank
    at = jnp.arange(n_leaf * cap, dtype=jnp.int32)[:, None] == place[None, :]
    which = jnp.sum(jnp.where(at, ids, 0), axis=1)
    where = jnp.sum(jnp.where(at, blocks % local + 1, 0), axis=1) - 1
    table = jnp.concatenate([which, where, blocks]).astype(jnp.int32)

    v = jnp.transpose(voltage, (1, 2, 0, 3)).reshape(panels, fields, width)
    s = jnp.transpose(source, (1, 2, 0, 3)).reshape(panels, fields, width)
    sep = jnp.transpose(separator_source, (1, 0, 2))
    n_piece = sep_rows * SPLIT
    any_spec = pl.BlockSpec(memory_space=pl.ANY)
    vmem = pl.BlockSpec(memory_space=pltpu.VMEM)
    smem = pl.BlockSpec(memory_space=pltpu.SMEM)
    V, DMA = pltpu.VMEM, pltpu.SemaphoreType.DMA
    square = (sep_rows, width, width)
    leaf_out, sep_out = pl.pallas_call(
        functools.partial(kernel, n_leaf, n_col, cap, extent_x, extent_y, sep_rows, halves),
        out_shape=(
            jax.ShapeDtypeStruct((panels, fields, width), F32),
            jax.ShapeDtypeStruct((sep_rows, fields, width), F32),
        ),
        in_specs=[smem, vmem, vmem, vmem, vmem] + [any_spec] * 4,
        out_specs=(vmem, vmem),
        scratch_shapes=[
            V((panels, width, width), BF16), V((panels, width, width), BF16),
            V(square, F32), V(square, F32),
            V(square, BF16), V(square, BF16), V(square, BF16), V(square, BF16),
            V((panels, fields, width), BF16), V((entries, fields, block), F32),
            V((2, fields, 128), BF16), V((2, fields, 128), BF16),
            V((2, extent_y, fields, width), BF16),
            V((chips, local, fields, block), PAIR), V((chips, local, fields, block), PAIR),
            V((chips, local, fields, block), F32),
            V((chips, local, fields, block), BF16), V((chips, local, fields, block), BF16),
            V((sep_rows, fields, width), F32),
            V((n_piece, fields // SPLIT, width), BF16), V((n_piece, fields // SPLIT, width), BF16),
            V((sep_rows, fields, width), F32),
            V((n_piece, fields // SPLIT, width), HOP), V((n_piece, fields // SPLIT, width), HOP),
            V((n_leaf * local, fields, block), BF16),
            DMA((4,)), DMA((2,)), DMA((2,)), DMA((2,)), DMA((2,)),
            DMA((chips,)), DMA((chips,)), DMA((chips,)), DMA((chips,)),
            DMA((n_piece,)), DMA((n_piece,)), DMA((n_piece,)), DMA((n_piece,)),
            DMA((chips, sep_rows)), DMA((chips, sep_rows)),
            DMA((chips, sep_rows)), DMA((chips, sep_rows)),
        ],
        compiler_params=pltpu.CompilerParams(
            collective_id=0, has_side_effects=True, vmem_limit_bytes=56 * 2**20
        ),
    )(
        table, v, s, conduct.reshape(panels, width), sep,
        leaf_inverse.reshape(panels, width, width), update_matrix.reshape(panels, width, width),
        separator_inverse, separator_coupling,
    )
    leaf_result = jnp.transpose(
        leaf_out.reshape(extent_x, extent_y, fields, width), (2, 0, 1, 3)
    )
    return (leaf_result, jnp.transpose(sep_out, (1, 0, 2)))


def solution(mesh):
    placed = (
        P(None, "leaf", None, "col"),
        P(None, "leaf", None, "col"),
        P("leaf", None, "col"),
        P("leaf", None, "col", None),
        P("col", "leaf", None, None),
        P("leaf", None, None, "col"),
        P(),
        P(None, "leaf", "col"),
        P("leaf", "col", None),
        P("leaf", "col", None),
    )
    return jax.shard_map(
        body,
        mesh=mesh,
        in_specs=placed,
        out_specs=(P(None, "leaf", None, "col"), P(None, "leaf", "col")),
        check_vma=False,
    )
```

```python
import functools
import jax
import jax.numpy as jnp
from jax import lax
from jax.experimental import pallas as pl
from jax.experimental.pallas import tpu as pltpu
from jax.sharding import PartitionSpec as P

F32 = jnp.float32
BF16 = jnp.bfloat16
SPLIT = 2
PAIR = F32
HOP = BF16
NT = (((1,), (1,)), ((), ()))
NN = (((1,), (0,)), ((), ()))


def flipped(value, bits, count):
    total = 0
    weight = 1
    while weight < count:
        digit = (value // weight) % 2
        total = total + weight * (1 - digit if (bits // weight) % 2 else digit)
        weight *= 2
    return total


def dot(left, right, dims):
    return lax.dot_general(left, right, dims, preferred_element_type=F32)


def halved(value):
    high = value.astype(BF16)
    return high, (value - high.astype(F32)).astype(BF16)


def kernel(
    n_leaf, n_col, cap, extent_x, extent_y, sep_rows, halves,
    tab, v, s, cond, sep, inv_hbm, upd_hbm, sinv_hbm, coup_hbm,
    ls_hbm, res, gath_hbm,
    out, inv, upd, sinv, coup, c_hi, c_lo, d_hi, d_lo,
    resid, contrib, z_send, z_recv, x_recv,
    pair_send, pair_recv, keep, chip_send, chip_recv,
    drive, f_send, f_recv, scaled, b_send, b_recv, gath,
    load_sem, zs_sem, zr_sem, xs_sem, xr_sem, ps_sem, pr_sem, cs_sem, cr_sem,
    fs_sem, fr_sem, bs_sem, br_sem, gs_sem, gr_sem, hs_sem, hr_sem,
):
    panels, fields, width = v.shape
    block = width // halves
    local = sep_rows * halves
    chips = n_leaf // 2
    leaf = lax.axis_index("leaf")
    col = lax.axis_index("col")
    core = leaf % 2
    chip = leaf // 2
    sibling = chip * 2 + (1 - core)
    entries = 2 * panels
    owners_cap = n_leaf * cap
    MESH = pl.DeviceIdType.MESH

    def remote(src, dst, send, recv, target):
        return pltpu.make_async_remote_copy(
            src_ref=src, dst_ref=dst, send_sem=send, recv_sem=recv,
            device_id=target, device_id_type=MESH,
        )

    loads = [
        pltpu.make_async_copy(src, dst, load_sem.at[i])
        for i, (src, dst) in enumerate(
            ((upd_hbm, upd), (inv_hbm, inv), (coup_hbm, coup), (sinv_hbm, sinv))
        )
    ]
    for load in loads:
        load.start()

    barrier = pltpu.get_barrier_semaphore()
    for step in range(1, n_leaf):
        pl.semaphore_signal(
            barrier, inc=1, device_id={"leaf": (leaf + step) % n_leaf}, device_id_type=MESH
        )
    has_below, has_above = col > 0, col < n_col - 1
    leaf_below, leaf_above = leaf > 0, leaf < n_leaf - 1

    @pl.when(has_below)
    def _():
        pl.semaphore_signal(barrier, inc=1, device_id={"col": col - 1}, device_id_type=MESH)

    @pl.when(has_above)
    def _():
        pl.semaphore_signal(barrier, inc=1, device_id={"col": col + 1}, device_id_type=MESH)

    lane = lax.broadcasted_iota(jnp.int32, (fields, 128), 1)
    first = jnp.zeros((fields, 128), F32)
    last = jnp.zeros((fields, 128), F32)
    for p in range(panels):
        first = jnp.where(lane == p, v[p, :, 0:128].astype(F32)[:, 0:1], first)
        last = jnp.where(lane == p, v[p, :, width - 128:].astype(F32)[:, 127:128], last)
    z_send[0] = first.astype(BF16)
    z_send[1] = last.astype(BF16)

    beside_col = (col + n_col - 1) // n_col + (2 * n_col - 2 - col) // n_col
    pl.semaphore_wait(barrier, n_leaf - 1 + beside_col)

    z_down = lambda: remote(z_send.at[0], z_recv.at[1], zs_sem.at[0], zr_sem.at[1], {"col": col - 1})
    z_up = lambda: remote(z_send.at[1], z_recv.at[0], zs_sem.at[1], zr_sem.at[0], {"col": col + 1})
    x_down = lambda: remote(
        v.at[pl.ds(0, extent_y)], x_recv.at[1], xs_sem.at[0], xr_sem.at[1], {"leaf": leaf - 1}
    )
    x_up = lambda: remote(
        v.at[pl.ds(panels - extent_y, extent_y)], x_recv.at[0], xs_sem.at[1], xr_sem.at[0],
        {"leaf": leaf + 1},
    )

    for has, copy in ((has_below, z_down), (has_above, z_up), (leaf_below, x_down), (leaf_above, x_up)):
        @pl.when(has)
        def _(copy=copy):
            copy().start()

    for has, ref, slot in (
        (has_below, z_recv, 0), (has_above, z_recv, 1), (leaf_below, x_recv, 0), (leaf_above, x_recv, 1),
    ):
        @pl.when(jnp.logical_not(has))
        def _(ref=ref, slot=slot):
            ref[slot] = jnp.zeros(ref.shape[1:], ref.dtype)

    @pl.when(has_below)
    def _():
        z_up().wait_recv()

    @pl.when(has_above)
    def _():
        z_down().wait_recv()

    loads[0].wait()
    wide_lane = lax.broadcasted_iota(jnp.int32, (fields, width), 1)

    def residual_panel(x, y):
        p = x * extent_y + y
        center = v[p].astype(F32)
        before = z_recv[0].astype(F32)[:, p:p + 1]
        after = z_recv[1].astype(F32)[:, p:p + 1]
        beside = jnp.where(wide_lane == 0, before, pltpu.roll(center, 1, 1))
        beside = beside + jnp.where(wide_lane == width - 1, after, pltpu.roll(center, width - 1, 1))
        beside = beside + (v[p - extent_y] if x > 0 else x_recv[0, y]).astype(F32)
        beside = beside + (v[p + extent_y] if x < extent_x - 1 else x_recv[1, y]).astype(F32)
        if y > 0:
            beside = beside + v[p - 1].astype(F32)
        if y < extent_y - 1:
            beside = beside + v[p + 1].astype(F32)
        low = (s[p].astype(F32) - ((6.0 + cond[x, y:y + 1, :]) * center - beside)).astype(BF16)
        resid[p] = low
        product = dot(low, upd[p], NT)
        contrib[2 * p] = product[:, :block]
        contrib[2 * p + 1] = product[:, block:]

    for x in range(1, extent_x - 1):
        for y in range(extent_y):
            residual_panel(x, y)

    @pl.when(leaf_below)
    def _():
        x_up().wait_recv()

    @pl.when(leaf_above)
    def _():
        x_down().wait_recv()

    for x in (0, extent_x - 1):
        for y in range(extent_y):
            residual_panel(x, y)

    def dense(owner, m):
        total = jnp.zeros((fields, block), F32)
        for r in range(cap):
            at = owner * cap + r
            weight = jnp.where(tab[owners_cap + at] == m, 1.0, 0.0).astype(F32)
            total = total + weight * contrib[tab[at]]
        return total

    order = list(range(chips - 1, -1, -1))
    peer_chip = [flipped(chip, d, chips) for d in range(chips)]

    def pair_copy(d):
        return remote(pair_send.at[d], pair_recv.at[d], ps_sem.at[d], pr_sem.at[d], {"leaf": sibling})

    def chip_copy(d):
        return remote(
            chip_send.at[d], chip_recv.at[d], cs_sem.at[d], cr_sem.at[d],
            {"leaf": peer_chip[d] * 2 + core},
        )

    for d in order:
        def fill(m, carry, d=d):
            pair_send[d, m] = dense(peer_chip[d] * 2 + (1 - core), m).astype(pair_send.dtype)
            return carry
        lax.fori_loop(0, local, fill, 0)
        pair_copy(d).start()
    for d in order:
        def fill_own(m, carry, d=d):
            keep[d, m] = dense(peer_chip[d] * 2 + core, m)
            return carry
        lax.fori_loop(0, local, fill_own, 0)
        pair_copy(d).wait_recv()
        if d > 0:
            chip_send[d] = (keep[d] + pair_recv[d].astype(F32)).astype(BF16)
            chip_copy(d).start()

    for load in loads[1:]:
        load.wait()

    def leaf_scale(p, carry):
        out[p] = dot(resid[p], inv[p], NT)
        return carry
    lax.fori_loop(0, panels, leaf_scale, 0)
    scaled_out = pltpu.make_async_copy(out, ls_hbm, load_sem.at[4])
    scaled_out.start()
    for e in range(sep_rows):
        c_hi[e], c_lo[e] = halved(coup[e])
        d_hi[e], d_lo[e] = halved(sinv[e])

    for e in range(sep_rows):
        for h in range(halves):
            m = e * halves + h
            lanes = slice(h * block, (h + 1) * block)
            drive[e, :, lanes] = sep[:, e, lanes] - (keep[0, m] + pair_recv[0, m].astype(F32))
    for d in order:
        if d > 0:
            chip_copy(d).wait_recv()
            for e in range(sep_rows):
                for h in range(halves):
                    lanes = slice(h * block, (h + 1) * block)
                    drive[e, :, lanes] = drive[e, :, lanes] - chip_recv[d, e * halves + h].astype(F32)

    rows_each = fields // SPLIT
    pieces = [(e, q) for e in range(sep_rows) for q in range(SPLIT)]

    def f_copy(i):
        return remote(f_send.at[i], f_recv.at[i], fs_sem.at[i], fr_sem.at[i], {"col": col + 1})

    def b_copy(i):
        return remote(b_send.at[i], b_recv.at[i], bs_sem.at[i], br_sem.at[i], {"col": col - 1})

    def spot(owner_leaf, e):
        return pl.ds((owner_leaf * sep_rows + e) * halves, halves)

    def gather_copy(d, e):
        here = gath.at[spot(leaf, e)]
        return remote(here, here, gs_sem.at[d, e], gr_sem.at[d, e], {"leaf": peer_chip[d] * 2 + core})

    def hand_copy(d, e):
        here = gath.at[spot(peer_chip[d] * 2 + core, e)]
        return remote(here, here, hs_sem.at[d, e], hr_sem.at[d, e], {"leaf": sibling})

    def scale(e, rows):
        high, low = halved(drive[e, rows])
        return dot(high, d_hi[e], NT) + dot(high, d_lo[e], NT) + dot(low, d_hi[e], NT)

    def settle(i, e, q, rows, value):
        low = value.astype(BF16)

        @pl.when(has_below)
        def _():
            rest = (value - low.astype(F32)).astype(BF16)
            up = dot(low, c_hi[e], NN) + dot(low, c_lo[e], NN) + dot(rest, c_hi[e], NN)
            b_send[i] = up.astype(b_send.dtype)
            b_copy(i).start()

        res[e, rows] = value
        for h in range(halves):
            gath[(leaf * sep_rows + e) * halves + h, rows] = low[:, h * block:(h + 1) * block]
        if q == SPLIT - 1:
            for d in order:
                if d > 0:
                    gather_copy(d, e).start()
            hand_copy(0, e).start()

    for i, (e, q) in enumerate(pieces):
        rows = slice(q * rows_each, (q + 1) * rows_each)

        @pl.when(has_below)
        def _(i=i, e=e, rows=rows):
            f_copy(i).wait_recv()
            drive[e, rows] = drive[e, rows] - (
                dot(f_recv[i], c_hi[e], NT) + dot(f_recv[i], c_lo[e], NT)
            )

        @pl.when(has_above)
        def _(i=i, e=e, rows=rows):
            f_send[i] = drive[e, rows].astype(BF16)
            f_copy(i).start()

        @pl.when(jnp.logical_not(has_above))
        def _(i=i, e=e, q=q, rows=rows):
            settle(i, e, q, rows, scale(e, rows))

    @pl.when(has_above)
    def _():
        for e in range(sep_rows):
            scaled[e] = scale(e, slice(None))
        for i, (e, q) in enumerate(pieces):
            rows = slice(q * rows_each, (q + 1) * rows_each)
            b_copy(i).wait_recv()
            settle(i, e, q, rows, scaled[e, rows] - b_recv[i].astype(F32))

    for e in range(sep_rows):
        for d in range(1, chips):
            gather_copy(d, e).wait_recv()
            hand_copy(d, e).start()
    for e in range(sep_rows):
        for d in range(chips):
            hand_copy(d, e).wait_recv()

    gath_out = pltpu.make_async_copy(gath, gath_hbm, load_sem.at[5])
    gath_out.start()
    for has, copy in ((has_below, z_down), (has_above, z_up), (leaf_below, x_down), (leaf_above, x_up)):
        @pl.when(has)
        def _(copy=copy):
            copy().wait_send()
    for i in range(len(pieces)):
        @pl.when(has_above)
        def _(i=i):
            f_copy(i).wait_send()

        @pl.when(has_below)
        def _(i=i):
            b_copy(i).wait_send()
    for d in range(chips):
        pair_copy(d).wait_send()
        if d > 0:
            chip_copy(d).wait_send()
        for e in range(sep_rows):
            hand_copy(d, e).wait_send()
            if d > 0:
                gather_copy(d, e).wait_send()
    scaled_out.wait()
    gath_out.wait()


def finish(start, tab, upd, gath, ls, out):
    extent_y, fields, width = ls.shape
    block = gath.shape[2]
    x = pl.program_id(0)
    for y in range(extent_y):
        at = start + 2 * (x * extent_y + y)
        total = dot(gath[tab[at]], upd[y, :block], NN) + dot(gath[tab[at + 1]], upd[y, block:], NN)
        out[:, 0, y, :] = ls[y] - total


def body(
    voltage,
    source,
    conduct,
    leaf_inverse,
    update_rows,
    update_matrix,
    chain_slot,
    separator_source,
    separator_inverse,
    separator_coupling,
):
    fields, extent_x, extent_y, width = voltage.shape
    per_leaf = update_rows.shape[3]
    block = update_matrix.shape[2] // per_leaf
    halves = width // block
    panels = extent_x * extent_y
    chains = chain_slot.shape[0]
    sep_rows = separator_source.shape[1]
    n_leaf, n_col = lax.axis_size("leaf"), lax.axis_size("col")
    chips = n_leaf // 2
    entries = panels * per_leaf
    cap = max(2, (entries + n_leaf - 1) // n_leaf)
    local = sep_rows * halves

    targets = update_rows.reshape(entries)
    hit = (targets // halves)[:, None] == jnp.arange(chains, dtype=jnp.int32)
    slots = jnp.sum(jnp.where(hit, chain_slot, 0), axis=1)
    blocks = slots * halves + targets % halves
    owner = slots // sep_rows
    ids = jnp.arange(entries, dtype=jnp.int32)
    earlier = (owner[:, None] == owner[None, :]) & (ids[None, :] < ids[:, None])
    rank = jnp.sum(earlier.astype(jnp.int32), axis=1)
    place = owner * cap + rank
    at = jnp.arange(n_leaf * cap, dtype=jnp.int32)[:, None] == place[None, :]
    which = jnp.sum(jnp.where(at, ids, 0), axis=1)
    where = jnp.sum(jnp.where(at, blocks % local + 1, 0), axis=1) - 1
    table = jnp.concatenate([which, where, blocks]).astype(jnp.int32)

    v = jnp.transpose(voltage, (1, 2, 0, 3)).reshape(panels, fields, width)
    s = jnp.transpose(source, (1, 2, 0, 3)).reshape(panels, fields, width)
    n_piece = sep_rows * SPLIT
    any_spec = pl.BlockSpec(memory_space=pl.ANY)
    vmem = pl.BlockSpec(memory_space=pltpu.VMEM)
    smem = pl.BlockSpec(memory_space=pltpu.SMEM)
    V, DMA = pltpu.VMEM, pltpu.SemaphoreType.DMA
    square = (sep_rows, width, width)
    ls, sep_out, gathered = pl.pallas_call(
        functools.partial(kernel, n_leaf, n_col, cap, extent_x, extent_y, sep_rows, halves),
        out_shape=(
            jax.ShapeDtypeStruct((panels, fields, width), F32),
            jax.ShapeDtypeStruct((sep_rows, fields, width), F32),
            jax.ShapeDtypeStruct((n_leaf * local, fields, block), BF16),
        ),
        in_specs=[smem, vmem, vmem, vmem, vmem] + [any_spec] * 4,
        out_specs=(any_spec, vmem, any_spec),
        scratch_shapes=[
            V((panels, fields, width), F32),
            V((panels, width, width), BF16), V((panels, width, width), BF16),
            V(square, F32), V(square, F32),
            V(square, BF16), V(square, BF16), V(square, BF16), V(square, BF16),
            V((panels, fields, width), BF16), V((entries, fields, block), F32),
            V((2, fields, 128), BF16), V((2, fields, 128), BF16),
            V((2, extent_y, fields, width), BF16),
            V((chips, local, fields, block), PAIR), V((chips, local, fields, block), PAIR),
            V((chips, local, fields, block), F32),
            V((chips, local, fields, block), BF16), V((chips, local, fields, block), BF16),
            V((sep_rows, fields, width), F32),
            V((n_piece, fields // SPLIT, width), BF16), V((n_piece, fields // SPLIT, width), BF16),
            V((sep_rows, fields, width), F32),
            V((n_piece, fields // SPLIT, width), HOP), V((n_piece, fields // SPLIT, width), HOP),
            V((n_leaf * local, fields, block), BF16),
            DMA((6,)), DMA((2,)), DMA((2,)), DMA((2,)), DMA((2,)),
            DMA((chips,)), DMA((chips,)), DMA((chips,)), DMA((chips,)),
            DMA((n_piece,)), DMA((n_piece,)), DMA((n_piece,)), DMA((n_piece,)),
            DMA((chips, sep_rows)), DMA((chips, sep_rows)),
            DMA((chips, sep_rows)), DMA((chips, sep_rows)),
        ],
        compiler_params=pltpu.CompilerParams(
            collective_id=0, has_side_effects=True, vmem_limit_bytes=56 * 2**20
        ),
    )(
        table, v, s, conduct, separator_source,
        leaf_inverse.reshape(panels, width, width), update_matrix.reshape(panels, width, width),
        separator_inverse, separator_coupling,
    )
    leaf_result = pl.pallas_call(
        functools.partial(finish, 2 * n_leaf * cap),
        out_shape=jax.ShapeDtypeStruct((fields, extent_x, extent_y, width), F32),
        grid=(extent_x,),
        in_specs=[
            smem,
            pl.BlockSpec((extent_y, width, width), lambda x: (x, 0, 0)),
            vmem,
            pl.BlockSpec((extent_y, fields, width), lambda x: (x, 0, 0)),
        ],
        out_specs=pl.BlockSpec((fields, 1, extent_y, width), lambda x: (0, x, 0, 0)),
        compiler_params=pltpu.CompilerParams(vmem_limit_bytes=56 * 2**20),
    )(table, update_matrix.reshape(panels, width, width), gathered, ls)
    return (leaf_result, jnp.transpose(sep_out, (1, 0, 2)))


def solution(mesh):
    placed = (
        P(None, "leaf", None, "col"),
        P(None, "leaf", None, "col"),
        P("leaf", None, "col"),
        P("leaf", None, "col", None),
        P("col", "leaf", None, None),
        P("leaf", None, None, "col"),
        P(),
        P(None, "leaf", "col"),
        P("leaf", "col", None),
        P("leaf", "col", None),
    )
    return jax.shard_map(
        body,
        mesh=mesh,
        in_specs=placed,
        out_specs=(P(None, "leaf", None, "col"), P(None, "leaf", "col")),
        check_vma=False,
    )
```
